512 devices in a mesh: row: 32 (over z_hi, y), col: 16 (over z_lo, x, core).
Axes of the slice: x: 4, y: 8, z: 8 (z_hi: 4, z_lo: 2; z = z_hi * 2 + z_lo), core: 2. Of those that a mesh axis runs over, the one named last changes fastest.
Arguments:
- blocks: bfloat16 [32, 16, 8, 256, 256], P('row', 'col'), may hold values from -0.875 to 0.875
- block_slots: int32 [32, 16, 8], P('row', 'col'), may hold values from 0 to 8, as said below
- density: bfloat16 [16384, 16384], P('row', 'col'), may hold values from -3 to 3
- branch: int32 [64], replicated, may hold values from 0 to 1
Outputs:
- purified: float32 [16384, 16384], P('row', 'col')
The draws below stay inside these ranges and needn't reach their ends.
Inputs may be any that keep to these rules, and one draw needn't show every extreme that they name: `block_slots`: in each tile the stored slots name distinct positions below 8; an empty slot holds 8; at least half of a tile's slots are stored.
All inputs are finite; a program needn't handle non-finite values.
Results may differ from the reference program's by a relative error of at most 0.0003.
Values may be sent and summed in bfloat16 or wider, within the bound.
No kernel may reach another device: no remote copies, remote signals or barrier semaphores. Data moves between devices by JAX's collectives and lax.ppermute only.
A program may use at most 64 MiB of HBM per device.

```python
import jax
import jax.numpy as jnp
from jax import lax

BLOCK = 256
ROW_SET = 4
COL_SET = 2
STEPS = 4
GRID = 16
LAYERS = 2
ROWS = 32
SLOT = 8
ORDER = 16384


def draw_block_slots(key, part):
    key = jax.random.fold_in(key, 11)
    count_key, order_key = jax.random.split(key)
    devices = ROWS * GRID
    device_keys = jax.random.split(order_key, devices)
    orders = jax.vmap(lambda single: jax.random.permutation(single, SLOT))(device_keys)
    stored = jax.random.randint(count_key, (devices,), SLOT // 2, SLOT + 1)
    stored = stored.at[0].set(SLOT).at[devices - 1].set(SLOT // 2)
    position = jnp.arange(SLOT, dtype=jnp.int32)[None, :]
    filled = jnp.where(position < stored[:, None], orders.astype(jnp.int32), SLOT)
    return filled.reshape(ROWS, GRID, SLOT).astype(jnp.int32)


def touch_ends(array, own_key, low, largest):
    place = [jax.random.randint(jax.random.fold_in(own_key, axis), (), 0, length) for axis, length in enumerate(array.shape)]
    longest = array.shape.index(max(array.shape))
    next_to = place[:longest] + [(place[longest] + 1) % array.shape[longest]] + place[longest + 1:]
    return array.at[tuple(place)].set(low).at[tuple(next_to)].set(largest)


def level_of(rng, extent, pieces, low, largest):
    def one(dim, blocks):
        heights = jax.random.uniform(jax.random.fold_in(jax.random.fold_in(rng, 6), dim), (blocks,), jnp.float32, low / len(pieces), largest / len(pieces))
        return jnp.repeat(jnp.exp(heights), extent[dim] // blocks).reshape((-1,) + (1,) * (len(extent) - dim - 1))

    factor_of = one(*pieces[0])
    for cut in pieces[1:]:
        factor_of = factor_of * one(*cut)
    return factor_of


def noise(own_key, shape, scale, reach, cuts=(), held_as=jnp.bfloat16):
    level = level_of(own_key, shape, cuts, -0.22, 0.18) if cuts else 1.0
    values = jax.random.normal(own_key, shape, jnp.float32) * scale * level
    return jnp.minimum(jnp.maximum(values, -reach), reach).astype(held_as)


def setup_inputs(seed: int = 0) -> dict:
    seeds = jax.random.split(jax.random.key(seed), 5)
    blocks = noise(seeds[0], (ROWS, GRID, SLOT, BLOCK, BLOCK), 0.15, 0.875, ((0, 32), (1, 16)))
    block_slots = draw_block_slots(jax.random.fold_in(seeds[4], 71), 0)
    density = noise(seeds[2], (ORDER, ORDER), 0.5, 3.0, ((0, 32), (1, 16)))
    branch = touch_ends(jax.random.randint(seeds[3], (ORDER // BLOCK,), 0, 2), jax.random.fold_in(seeds[3], 1), 0, 1).astype(jnp.int32)
    return {"blocks": blocks, "block_slots": block_slots, "density": density, "branch": branch}


def build_tile(blocks_dev, slots_dev):
    onehot = (slots_dev[:, None] == jnp.arange(SLOT, dtype=jnp.int32)[None, :]).astype(jnp.float32)
    onehot = onehot.reshape(SLOT, ROW_SET, COL_SET)
    placed = jnp.einsum("suq,sit->uiqt", onehot, blocks_dev.astype(jnp.float32), precision=lax.Precision.HIGHEST)
    return placed.reshape(ROW_SET * BLOCK, COL_SET * BLOCK).astype(jnp.bfloat16)


def reference(blocks, block_slots, density, branch):
    flat_blocks = blocks.reshape(ROWS * GRID, SLOT, BLOCK, BLOCK)
    flat_slots = block_slots.reshape(ROWS * GRID, SLOT)
    tiles_all = lax.map(lambda members: build_tile(members[0], members[1]), (flat_blocks, flat_slots))
    tiles_all = tiles_all.reshape(ROWS, GRID, ROW_SET * BLOCK, COL_SET * BLOCK)
    tile_rows = ROW_SET * BLOCK

    def one_tile(position):
        row_panel = position // GRID
        col_panel = position % GRID
        summed = jnp.zeros((tile_rows, tile_rows), jnp.float32)
        for layer_index in range(LAYERS):
            for section_index in range(STEPS):
                left_tile = tiles_all[row_panel * LAYERS + layer_index, (col_panel + section_index) % GRID]
                right_tile = tiles_all[col_panel * LAYERS + layer_index, (row_panel + section_index) % GRID]
                summed = summed + jnp.dot(left_tile, right_tile.T, preferred_element_type=jnp.float32)
        return summed

    products = lax.map(one_tile, jnp.arange(GRID * GRID, dtype=jnp.int32))
    product = products.reshape(GRID, GRID, tile_rows, tile_rows).transpose(0, 2, 1, 3).reshape(GRID * tile_rows, GRID * tile_rows)
    doubled = 2.0 * density.astype(jnp.float32) - product
    row_branch = jnp.repeat(branch, BLOCK)
    return jnp.where(row_branch[:, None] == 1, product, doubled)
```

```python
import jax
import jax.numpy as jnp
from jax import lax
from jax.sharding import PartitionSpec as P

BLOCK = 256
ROW_SET = 4
COL_SET = 2
STEPS = 4
SLOT = 8
CHUNKS = 2
LAYER_TYPE = jnp.float32


def place(flat):
    row, col = divmod(flat, 16)
    return row // 8, row % 8, col // 8, col % 8 // 2, col % 2


def index(zh, y, zl, x, core):
    return ((zh % 4) * 8 + y % 8) * 16 + zl * 8 + x * 2 + core


def move(value, where):
    pairs = [(i, where(*place(i))) for i in range(512)]
    return lax.ppermute(value, ("row", "col"), [p for p in pairs if p[1] is not None])


def along_y(value, by):
    return move(value, lambda zh, y, zl, x, core: index(zh, y + by, zl, x, core))


def mirror(value, flip):
    def where(zh, y, zl, x, core):
        return index(zl * 2 + x // 2, y, zh // 2, (zh % 2) * 2 + (x % 2 ^ flip // 2), core ^ flip % 2)

    return move(value, where)


def build_tile(blocks_dev, slots_dev):
    onehot = (slots_dev[:, None] == jnp.arange(SLOT, dtype=jnp.int32)[None, :]).astype(jnp.bfloat16)
    onehot = onehot.reshape(SLOT, ROW_SET, COL_SET)
    placed = jnp.einsum("suq,sit->uiqt", onehot, blocks_dev, preferred_element_type=jnp.float32)
    return placed.astype(jnp.bfloat16).reshape(ROW_SET * BLOCK, COL_SET * BLOCK)


def pick(stack, i):
    return lax.dynamic_index_in_dim(stack, i, 0, keepdims=False)


def body(blocks, block_slots, density, branch):
    row_place = lax.axis_index("row")
    col_place = lax.axis_index("col")
    layer = row_place % 2
    q = row_place // 2 % 4
    own = col_place % 4
    core = own % 2
    upper = own // 2
    tile = build_tile(blocks[0, 0], block_slots[0, 0])
    width = COL_SET * BLOCK
    quarters = tile.reshape(ROW_SET, BLOCK, width)
    span = BLOCK // CHUNKS
    half = span // 2

    windows = []
    for chunk in range(CHUNKS):
        part = quarters[:, chunk * span:(chunk + 1) * span]
        came = jnp.stack([mirror(pick(part, own ^ flip), flip) for flip in range(4)])
        held = jnp.stack([pick(came, own ^ j) for j in range(4)])
        following = move(held[:3], lambda zh, y, zl, x, core: index(zh - 1, y, zl, x, core))
        windows.append(jnp.concatenate([held, following]))

    near = lax.ppermute(tile, "col", [(i, i - 1) for i in range(1, 16, 2)])
    second = lax.ppermute(tile, "col", [(i, (i - 2) % 16) for i in range(16)])
    swapped = lax.ppermute(second, "col", [(i, i ^ 1) for i in range(16)])
    far = lax.ppermute(second, "col", [(i, (i - 1) % 16) for i in range(0, 16, 2)])
    first = jnp.where(core == 0, near, swapped)
    third = jnp.where(core == 0, swapped, far)
    left = jnp.concatenate([tile, first, second, third], axis=1)
    half_rows = left.shape[0] // 2
    left_kept = lax.dynamic_slice_in_dim(left, layer * half_rows, half_rows, 0)
    left_given = lax.dynamic_slice_in_dim(left, (1 - layer) * half_rows, half_rows, 0)

    outs = []
    for chunk in range(CHUNKS):
        window = windows[chunk]

        def view(shift):
            return lax.dynamic_slice_in_dim(window, (q + shift) % 4, 4, 0)

        ahead = along_y(jnp.concatenate([view(1), view(2)[:, :half]], axis=1), 2)
        back = along_y(jnp.concatenate([view(3), view(2)[:, half:]], axis=1), -2)
        ahead_two = along_y(ahead[:, span:], 2)
        back_two = along_y(back[:, span:], -2)
        mine = view(0)
        before, after = ahead[:, :span], back[:, :span]
        opposite = jnp.concatenate([ahead_two, back_two], axis=1)
        even = jnp.stack([mine, opposite])
        odd = jnp.stack([before, after])
        matches = core == q % 2
        kept = jnp.where(matches, even, odd)
        came = move(jnp.where(matches, odd, even), lambda zh, y, zl, x, core: index(zh, y, zl, x, core ^ 1))
        leading = jnp.where(matches, q, (q + 3) % 4) // 2
        chosen = jnp.where(leading == upper, 0, 1)
        stay = jnp.stack([pick(kept, chosen), pick(came, chosen)])
        leave = jnp.stack([pick(kept, 1 - chosen), pick(came, 1 - chosen)])
        other = move(leave, lambda zh, y, zl, x, core: index(zh, y, zl, x ^ 1, core))
        both = jnp.concatenate([stay, other])
        right = jnp.stack([pick(both, own ^ u) for u in range(4)])
        right = right.transpose(0, 2, 1, 3).reshape(ROW_SET * span, STEPS * width)

        def contract(rows):
            return lax.dot_general(rows, right, (((1,), (1,)), ((), ())), preferred_element_type=jnp.float32)

        given = contract(left_given).astype(LAYER_TYPE)
        received = move(given, lambda zh, y, zl, x, core: index(zh, y ^ 1, zl, x, core))
        summed = contract(left_kept) + received.astype(jnp.float32)
        outs.append(summed.reshape(half_rows, ROW_SET, span))
    summed = jnp.stack(outs, axis=2).reshape(half_rows, ROW_SET * BLOCK)
    block_count = half_rows // BLOCK
    local_branch = lax.dynamic_slice_in_dim(branch, row_place * block_count, block_count, 0)
    row_branch = jnp.repeat(local_branch, BLOCK)
    doubled = 2.0 * density.astype(jnp.float32) - summed
    return jnp.where(row_branch[:, None] == 1, summed, doubled)


def solution(mesh):
    in_specs = (P("row", "col", None, None, None), P("row", "col", None), P("row", "col"), P())
    out_specs = P("row", "col")
    return jax.shard_map(body, mesh=mesh, in_specs=in_specs, out_specs=out_specs, check_vma=False)
```

```python
import jax
import jax.numpy as jnp
from jax import lax
from jax.sharding import PartitionSpec as P

BLOCK = 256
ROW_SET = 4
COL_SET = 2
STEPS = 4
SLOT = 8
SPANS = (512, 512)
LAYER_TYPE = jnp.float16


def place(flat):
    row, col = divmod(flat, 16)
    return row // 8, row % 8, col // 8, col % 8 // 2, col % 2


def index(zh, y, zl, x, core):
    return ((zh % 4) * 8 + y % 8) * 16 + zl * 8 + x * 2 + core


def move(value, where):
    pairs = [(i, where(*place(i))) for i in range(512)]
    return lax.ppermute(value, ("row", "col"), [p for p in pairs if p[1] is not None])


def mirror(zh, y, zl, x, core):
    return index(zl * 2 + x // 2, y, zh // 2, zh % 2 * 2 + x % 2, core)


def mirror_before(zh, y, zl, x, core):
    if x % 2 * 2 + core == 3:
        return None
    return index(zl * 2 + x // 2 - 1, y, zh // 2, zh % 2 * 2 + x % 2, core)


def spread(turn):
    def where(zh, y, zl, x, core):
        q, low = y // 2, x % 2 * 2 + core
        to = (q + (x % 2 + core * 2 ^ turn)) % 4
        return index(zh, to * 2 + y % 2, zl, x // 2 * 2 + q // 2, q % 2)

    return where


def build_tile(blocks_dev, slots_dev):
    onehot = (slots_dev[:, None] == jnp.arange(SLOT, dtype=jnp.int32)[None, :]).astype(jnp.bfloat16)
    onehot = onehot.reshape(SLOT, ROW_SET, COL_SET)
    placed = jnp.einsum("suq,sit->uiqt", onehot, blocks_dev, preferred_element_type=jnp.float32)
    return placed.astype(jnp.bfloat16).reshape(ROW_SET * BLOCK, COL_SET * BLOCK)


def body(blocks, block_slots, density, branch):
    row_place = lax.axis_index("row")
    col_place = lax.axis_index("col")
    layer = row_place % 2
    q = row_place // 2 % 4
    low = col_place % 4
    core = col_place % 2
    tile = build_tile(blocks[0, 0], block_slots[0, 0])
    rows = tile.shape[0]
    half = rows // 2

    parts = [tile[sum(SPANS[:k]) * BLOCK // 256:sum(SPANS[:k + 1]) * BLOCK // 256] for k in range(len(SPANS))]

    def both(part):
        return move(part, mirror), move(part, mirror_before)

    def turned(value):
        return value // 2 + value % 2 * 2

    rights = []
    held = both(parts[0])
    for chunk in range(len(parts)):
        coming = both(lax.optimization_barrier((parts[chunk + 1], held))[0]) if chunk + 1 < len(parts) else None
        for turn in range(4):
            to = (q + (turned(low) ^ turn)) % 4
            chosen = jnp.where(to <= low, *held)
            if len(rights) > 2:
                chosen, rights[-3] = lax.optimization_barrier((chosen, rights[-3]))
            rights.append(move(chosen, spread(turn)))
        held = coming

    second = lax.ppermute(tile, "col", [(i, (i - 2) % 16) for i in range(16)])
    swapped = lax.ppermute(second, "col", [(i, i ^ 1) for i in range(16)])
    beside = lax.ppermute(jnp.where(core == 1, tile, second), "col", [(i, (i - 1) % 16) for i in range(16)])
    first = jnp.where(core == 0, beside, swapped)
    third = jnp.where(core == 0, swapped, beside)
    left = jnp.stack([tile, first, second, third])
    steps = [(turned((q - low) % 4 ^ turn) - q) % 4 for turn in range(4)]

    def left_rows(place):
        return [lax.dynamic_slice(left, (s, place * half, 0), (1, half, left.shape[2]))[0] for s in steps]

    left_given = left_rows(1 - layer)
    left_kept = left_rows(layer)

    def contract(lefts, rights):
        total = None
        for a, b in zip(lefts, rights):
            term = lax.dot_general(a, b, (((1,), (1,)), ((), ())), preferred_element_type=jnp.float32)
            total = term if total is None else total + term
        return total

    outs = []
    for chunk in range(len(parts)):
        came = rights[chunk * 4:chunk * 4 + 4]
        given = contract(left_given, came).astype(LAYER_TYPE)
        received = move(given, lambda zh, y, zl, x, core: index(zh, y ^ 1, zl, x, core))
        outs.append(contract(left_kept, came) + received.astype(jnp.float32))
    summed = jnp.concatenate(outs, axis=1)
    block_count = half // BLOCK
    local_branch = lax.dynamic_slice_in_dim(branch, row_place * block_count, block_count, 0)
    row_branch = jnp.repeat(local_branch, BLOCK)
    doubled = 2.0 * density.astype(jnp.float32) - summed
    return jnp.where(row_branch[:, None] == 1, summed, doubled)


def solution(mesh):
    in_specs = (P("row", "col", None, None, None), P("row", "col", None), P("row", "col"), P())
    out_specs = P("row", "col")
    return jax.shard_map(body, mesh=mesh, in_specs=in_specs, out_specs=out_specs, check_vma=False)
```

```python
import jax
import jax.numpy as jnp
from jax import lax
from jax.sharding import PartitionSpec as P

BLOCK = 256
ROW_SET = 4
COL_SET = 2
STEPS = 4
SLOT = 8
SPANS = (256, 384, 384)
LAYER_TYPE = jnp.float16


def place(flat):
    row, col = divmod(flat, 16)
    return row // 8, row % 8, col // 8, col % 8 // 2, col % 2


def index(zh, y, zl, x, core):
    return ((zh % 4) * 8 + y % 8) * 16 + zl * 8 + x * 2 + core


def move(value, where):
    pairs = [(i, where(*place(i))) for i in range(512)]
    return lax.ppermute(value, ("row", "col"), [p for p in pairs if p[1] is not None])


def mirror(zh, y, zl, x, core):
    return index(zl * 2 + x // 2, y, zh // 2, zh % 2 * 2 + x % 2, core)


def mirror_before(zh, y, zl, x, core):
    if x % 2 * 2 + core == 3:
        return None
    return index(zl * 2 + x // 2 - 1, y, zh // 2, zh % 2 * 2 + x % 2, core)


def spread(turn):
    def where(zh, y, zl, x, core):
        q, low = y // 2, x % 2 * 2 + core
        to = (q + (x % 2 + core * 2 ^ turn)) % 4
        return index(zh, to * 2 + y % 2, zl, x // 2 * 2 + q // 2, q % 2)

    return where


def build_tile(blocks_dev, slots_dev):
    onehot = (slots_dev[:, None] == jnp.arange(SLOT, dtype=jnp.int32)[None, :]).astype(jnp.bfloat16)
    onehot = onehot.reshape(SLOT, ROW_SET, COL_SET)
    placed = jnp.einsum("suq,sit->uiqt", onehot, blocks_dev, preferred_element_type=jnp.float32)
    return placed.astype(jnp.bfloat16).reshape(ROW_SET * BLOCK, COL_SET * BLOCK)


def body(blocks, block_slots, density, branch):
    row_place = lax.axis_index("row")
    col_place = lax.axis_index("col")
    layer = row_place % 2
    q = row_place // 2 % 4
    low = col_place % 4
    core = col_place % 2
    tile = build_tile(blocks[0, 0], block_slots[0, 0])
    rows = tile.shape[0]
    half = rows // 2

    parts = [tile[sum(SPANS[:k]) * BLOCK // 256:sum(SPANS[:k + 1]) * BLOCK // 256] for k in range(len(SPANS))]

    def both(part):
        return move(part, mirror), move(part, mirror_before)

    def turned(value):
        return value // 2 + value % 2 * 2

    rights = []
    held = both(parts[0])
    for chunk in range(len(parts)):
        coming = both(lax.optimization_barrier((parts[chunk + 1], held))[0]) if chunk + 1 < len(parts) else None
        for turn in range(4):
            to = (q + (turned(low) ^ turn)) % 4
            chosen = jnp.where(to <= low, *held)
            if len(rights) > 2:
                chosen, rights[-3] = lax.optimization_barrier((chosen, rights[-3]))
            rights.append(move(chosen, spread(turn)))
        held = coming

    second = lax.ppermute(tile, "col", [(i, (i - 2) % 16) for i in range(16)])
    swapped = lax.ppermute(second, "col", [(i, i ^ 1) for i in range(16)])
    beside = lax.ppermute(jnp.where(core == 1, tile, second), "col", [(i, (i - 1) % 16) for i in range(16)])
    first = jnp.where(core == 0, beside, swapped)
    third = jnp.where(core == 0, swapped, beside)
    left = jnp.stack([tile, first, second, third])
    steps = [(turned((q - low) % 4 ^ turn) - q) % 4 for turn in range(4)]

    def left_rows(place):
        return [lax.dynamic_slice(left, (s, place * half, 0), (1, half, left.shape[2]))[0] for s in steps]

    left_given = left_rows(1 - layer)
    left_kept = left_rows(layer)

    def contract(lefts, rights):
        total = None
        for a, b in zip(lefts, rights):
            term = lax.dot_general(a, b, (((1,), (1,)), ((), ())), preferred_element_type=jnp.float32)
            total = term if total is None else total + term
        return total

    outs = []
    for chunk in range(len(parts)):
        came = rights[chunk * 4:chunk * 4 + 4]
        given = contract(left_given, came).astype(LAYER_TYPE)
        received = move(given, lambda zh, y, zl, x, core: index(zh, y ^ 1, zl, x, core))
        outs.append(contract(left_kept, came) + received.astype(jnp.float32))
    summed = jnp.concatenate(outs, axis=1)
    block_count = half // BLOCK
    local_branch = lax.dynamic_slice_in_dim(branch, row_place * block_count, block_count, 0)
    row_branch = jnp.repeat(local_branch, BLOCK)
    doubled = 2.0 * density.astype(jnp.float32) - summed
    return jnp.where(row_branch[:, None] == 1, summed, doubled)


def solution(mesh):
    in_specs = (P("row", "col", None, None, None), P("row", "col", None), P("row", "col"), P())
    out_specs = P("row", "col")
    return jax.shard_map(body, mesh=mesh, in_specs=in_specs, out_specs=out_specs, check_vma=False)
```

```python
import jax
import jax.numpy as jnp
from jax import lax
from jax.sharding import PartitionSpec as P

BLOCK = 256
ROW_SET = 4
COL_SET = 2
STEPS = 4
SLOT = 8
SPANS = (256, 384, 384)
LAYER_TYPE = jnp.float16


def place(flat):
    row, col = divmod(flat, 16)
    return row // 8, row % 8, col // 8, col % 8 // 2, col % 2


def index(zh, y, zl, x, core):
    return ((zh % 4) * 8 + y % 8) * 16 + zl * 8 + x * 2 + core


def move(value, where):
    pairs = [(i, where(*place(i))) for i in range(512)]
    return lax.ppermute(value, ("row", "col"), [p for p in pairs if p[1] is not None])


def mirror(zh, y, zl, x, core):
    return index(zl * 2 + x // 2, y, zh // 2, zh % 2 * 2 + x % 2, core)


def mirror_before(zh, y, zl, x, core):
    if x % 2 * 2 + core == 3:
        return None
    return index(zl * 2 + x // 2 - 1, y, zh // 2, zh % 2 * 2 + x % 2, core)


def spread(turn):
    def where(zh, y, zl, x, core):
        q, low = y // 2, x % 2 * 2 + core
        to = (q + (x % 2 + core * 2 ^ turn)) % 4
        return index(zh, to * 2 + y % 2, zl, x // 2 * 2 + q // 2, q % 2)

    return where


def build_tile(blocks_dev, slots_dev):
    onehot = (slots_dev[:, None] == jnp.arange(SLOT, dtype=jnp.int32)[None, :]).astype(jnp.bfloat16)
    onehot = onehot.reshape(SLOT, ROW_SET, COL_SET)
    placed = jnp.einsum("suq,sit->uiqt", onehot, blocks_dev, preferred_element_type=jnp.float32)
    return placed.astype(jnp.bfloat16).reshape(ROW_SET * BLOCK, COL_SET * BLOCK)


def body(blocks, block_slots, density, branch):
    row_place = lax.axis_index("row")
    col_place = lax.axis_index("col")
    layer = row_place % 2
    q = row_place // 2 % 4
    low = col_place % 4
    core = col_place % 2
    tile = build_tile(blocks[0, 0], block_slots[0, 0])
    rows = tile.shape[0]
    half = rows // 2

    parts = [tile[sum(SPANS[:k]) * BLOCK // 256:sum(SPANS[:k + 1]) * BLOCK // 256] for k in range(len(SPANS))]

    def both(part):
        return move(part, mirror), move(part, mirror_before)

    def turned(value):
        return value // 2 + value % 2 * 2

    rights = []
    held = both(parts[0])
    for chunk in range(len(parts)):
        coming = both(lax.optimization_barrier((parts[chunk + 1], held))[0]) if chunk + 1 < len(parts) else None
        for turn in range(4):
            to = (q + (turned(low) ^ turn)) % 4
            chosen = jnp.where(to <= low, *held)
            if len(rights) > 2:
                chosen, rights[-3] = lax.optimization_barrier((chosen, rights[-3]))
            rights.append(move(chosen, spread(turn)))
        held = coming

    second = lax.ppermute(tile, "col", [(i, (i - 2) % 16) for i in range(16)])
    swapped = lax.ppermute(second, "col", [(i, i ^ 1) for i in range(16)])
    beside = lax.ppermute(jnp.where(core == 1, tile, second), "col", [(i, (i - 1) % 16) for i in range(16)])
    first = jnp.where(core == 0, beside, swapped)
    third = jnp.where(core == 0, swapped, beside)
    left = jnp.stack([tile, first, second, third])
    steps = [(turned((q - low) % 4 ^ turn) - q) % 4 for turn in range(4)]

    def left_rows(place):
        return [lax.dynamic_slice(left, (s, place * half, 0), (1, half, left.shape[2]))[0] for s in steps]

    left_given = left_rows(1 - layer)
    left_kept = left_rows(layer)

    def contract(lefts, rights):
        total = None
        for a, b in zip(lefts, rights):
            term = lax.dot_general(a, b, (((1,), (1,)), ((), ())), preferred_element_type=jnp.float32)
            total = term if total is None else total + term
        return total

    block_count = half // BLOCK
    local_branch = lax.dynamic_slice_in_dim(branch, row_place * block_count, block_count, 0)
    row_branch = jnp.repeat(local_branch, BLOCK)[:, None] == 1
    outs, begin = [], 0
    for chunk in range(len(parts)):
        came = rights[chunk * 4:chunk * 4 + 4]
        given = contract(left_given, came).astype(LAYER_TYPE)
        received = move(given, lambda zh, y, zl, x, core: index(zh, y ^ 1, zl, x, core))
        summed = contract(left_kept, came) + received.astype(jnp.float32)
        end = begin + summed.shape[1]
        doubled = 2.0 * density[:, begin:end].astype(jnp.float32) - summed
        outs.append(jnp.where(row_branch, summed, doubled))
        begin = end
    return jnp.concatenate(outs, axis=1)


def solution(mesh):
    in_specs = (P("row", "col", None, None, None), P("row", "col", None), P("row", "col"), P())
    out_specs = P("row", "col")
    return jax.shard_map(body, mesh=mesh, in_specs=in_specs, out_specs=out_specs, check_vma=False)
```
